32 devices in a mesh: runs: 2 (over y), gx: 4 (over z), gy: 2 (over x), gz: 2 (over core).
Axes of the slice: x: 2, y: 2, z: 4, core: 2. Of those that a mesh axis runs over, the one named last changes fastest.
Arguments:
- offsets: float32 [3, 32768], P(None, ('runs', 'gx', 'gy', 'gz')), parts along dimension 1, may hold values from -0.5 to 0.5
- particle_mass: float32 [32768], P(('runs', 'gx', 'gy', 'gz')), parts along dimension 0, may hold values from 0.5 to 2
- velocity: float32 [3, 32768], P(None, ('runs', 'gx', 'gy', 'gz')), parts along dimension 1, may hold values from -6 to 6
- home_cell: int32 [32768], P(('runs', 'gx', 'gy', 'gz')), parts along dimension 0, may hold values from 0 to 4095
- home_tile: int32 [32768], P(('runs', 'gx', 'gy', 'gz')), parts along dimension 0, may hold values from 0 to 7, as said below
- conv1_weight: bfloat16 [16, 4, 3, 3, 3], replicated, may hold values from -2.5 to 2.5
- conv1_bias: float32 [16], replicated, may hold values from -3 to 3
- conv2_weight: bfloat16 [16, 16, 3, 3, 3], replicated, may hold values from -0.3125 to 0.3125
- conv2_bias: float32 [16], replicated, may hold values from -3 to 3
- head_weight: bfloat16 [3, 16], replicated, may hold values from -1.5 to 1.5
Outputs:
- forces: float32 [3, 32768], P(None, ('runs', 'gx', 'gy', 'gz')), parts along dimension 1
The draws below stay inside these ranges and needn't reach their ends.
There are 2 independent parts, one for each index of `runs`. The reference program is written for one: setup_inputs(seed, part) draws one part's arguments, and reference() takes and returns one part's arrays. A program takes and returns all parts, laid end to end along the dimension named above; an argument that names none is the same for every part. Nothing has to cross between parts.
Inputs may be any that keep to these rules, and one draw needn't show every extreme that they name: `home_tile`: within the rows of one device (aligned blocks of 1024 rows) no tile is named more than 256 times; in every draw one tile is named exactly 256 times in every block.
All inputs are finite; a program needn't handle non-finite values.
Results may differ from the reference program's by a relative error of at most 0.0057.
Values may be sent and summed in bfloat16 or wider, within the bound.
A program may use at most 64 MiB of HBM per device.

```python
import math
import jax
import jax.numpy as jnp
from jax import lax

CH = 16
PAINTED = 4
TX = 16
TY = 128
TZ = 2
PDEV = 1024
NTILE = 8
TILE_COLS = 2
LEVELS = 2
CAP = 256
NX = 64
NY = 256
NZ = 4
PARTICLES = 16384


def draw_home_tile(key, part):
    block_rows = PARTICLES // PDEV
    hot_tile = jax.random.randint(jax.random.fold_in(key, 7), (), 0, NTILE).astype(jnp.int32)
    block_keys = jax.random.split(jax.random.fold_in(key, 11), block_rows)

    def one_block(block_key):
        key_pick, key_order = jax.random.split(block_key)
        chosen = jax.random.permutation(key_pick, (NTILE - 1) * CAP)[:PDEV - CAP].astype(jnp.int32)
        spread = chosen // CAP
        spread = spread + (spread >= hot_tile).astype(jnp.int32)
        gathered = jnp.concatenate([jnp.zeros((CAP,), jnp.int32) + hot_tile, spread])
        return gathered[jax.random.permutation(key_order, PDEV)]
    return jax.vmap(one_block)(block_keys).reshape(-1).astype(jnp.int32)


def set_ends(values, stream_key, low, largest):
    longest = values.shape.index(max(values.shape))
    spots = []
    for shift in (0, 1):
        where = [jax.random.randint(jax.random.fold_in(stream_key, axis), (), 0, length) for axis, length in enumerate(values.shape)]
        where[longest] = (where[longest] + shift) % values.shape[longest]
        spots.append(tuple(where))
    return values.at[spots[0]].set(low).at[spots[1]].set(largest)


def block_levels(rng, shape, cuts, smallest, high):
    def one(dim, parts):
        steps = jax.random.uniform(jax.random.fold_in(jax.random.fold_in(rng, 6), dim), (parts,), jnp.float32, smallest / len(cuts), high / len(cuts))
        return jnp.repeat(jnp.exp(steps), shape[dim] // parts).reshape((-1,) + (1,) * (len(shape) - dim - 1))

    factor_of = one(*cuts[0])
    for cut in cuts[1:]:
        factor_of = factor_of * one(*cut)
    return factor_of


def normal_values(stream_key, dims, deviation, limit, shards=(), kind=jnp.bfloat16):
    array = jax.random.normal(stream_key, dims, jnp.float32) * deviation
    if len(shards) > 0:
        array = block_levels(stream_key, dims, shards, -0.22, 0.18) * array
    return jnp.clip(array, min=-limit, max=limit).astype(kind)


def setup_inputs(seed: int = 0, part: int = 0) -> dict:
    keys = jax.random.split(jax.random.key(seed), 11)
    part_splits = jax.random.split(jax.random.fold_in(keys[10], part), 11)
    offsets = jnp.clip(jax.random.uniform(part_splits[0], (3, PARTICLES), jnp.float32, -0.5, 0.5) * block_levels(part_splits[0], (3, PARTICLES), ((1, 16),), -0.4, 0.0), -0.5, 0.5)
    particle_mass = jnp.clip(jnp.exp(math.log(2.0) - 1.3862944 * jax.random.uniform(part_splits[1], (PARTICLES,), jnp.float32) ** block_levels(part_splits[1], (PARTICLES,), ((0, 16),), -0.2, 0.2)), 0.5, 2.0)
    velocity = normal_values(part_splits[2], (3, PARTICLES), 1.0, 6.0, ((1, 16),), jnp.float32)
    home_cell = set_ends(jax.random.randint(part_splits[3], (PARTICLES,), 0, TZ * TX * TY), jax.random.fold_in(part_splits[3], 1), 0, (TZ * TX * TY) - 1).astype(jnp.int32)
    home_tile = draw_home_tile(jax.random.fold_in(jax.random.fold_in(keys[10], part), 71), part)
    conv1_weight = normal_values(keys[5], (CH, PAINTED, 3, 3, 3), 6 ** -0.5, 2.5)
    conv1_bias = normal_values(keys[6], (CH,), 0.5, 3.0, (), jnp.float32)
    conv2_weight = normal_values(keys[7], (CH, CH, 3, 3, 3), (27 * CH) ** -0.5, 0.3125)
    conv2_bias = normal_values(keys[8], (CH,), 0.5, 3.0, (), jnp.float32)
    head_weight = normal_values(keys[9], (3, CH), CH ** -0.5, 1.5)
    return dict(offsets=offsets, particle_mass=particle_mass, velocity=velocity, home_cell=home_cell, home_tile=home_tile, conv1_weight=conv1_weight, conv1_bias=conv1_bias, conv2_weight=conv2_weight, conv2_bias=conv2_bias, head_weight=head_weight)


def particle_cells(home_cell, home_tile):
    total_rows = home_cell.shape[0]
    holder = jnp.arange(total_rows, dtype=jnp.int32) // PDEV
    plane_group = holder % LEVELS
    tile_row = home_tile // TILE_COLS
    tile_column = home_tile % TILE_COLS
    local_z = home_cell // (TX * TY)
    local_x = (home_cell // TY) % TX
    local_y = home_cell % TY
    return (plane_group * TZ + local_z, tile_row * TX + local_x, tile_column * TY + local_y)


def axis_pair(base, fraction):
    step_dir = jnp.where(fraction >= 0.0, 1, -1).astype(jnp.int32)
    return (base, base + step_dir), (1.0 - jnp.abs(fraction), jnp.abs(fraction))


def corner_list(positions, offsets):
    z_pair, z_weight = axis_pair(positions[0], offsets[0])
    x_pair, x_weight = axis_pair(positions[1], offsets[1])
    y_pair, y_weight = axis_pair(positions[2], offsets[2])
    result = []
    for pick_z in range(2):
        for pick_x in range(2):
            for pick_y in range(2):
                plane_at = z_pair[pick_z]
                inside = ((plane_at >= 0) & (plane_at < NZ)).astype(jnp.float32)
                weight = z_weight[pick_z] * x_weight[pick_x] * y_weight[pick_y] * inside
                flat_index = (jnp.clip(plane_at, 0, NZ - 1) * NX + x_pair[pick_x] % NX) * NY + y_pair[pick_y] % NY
                result.append((flat_index.astype(jnp.int32), weight))
    return result


def convolve_all(mesh_field, weight, bias_vec, head_weight):
    padded = jnp.pad(mesh_field, ((0, 0), (1, 1), (0, 0), (0, 0)))
    padded = jnp.pad(padded, ((0, 0), (0, 0), (1, 1), (1, 1)), mode="wrap")

    def one_plane(plane_index):
        slab_part = lax.dynamic_slice_in_dim(padded, plane_index, 3, 1).astype(jnp.float32)
        summed = lax.conv_general_dilated(slab_part[None], weight.astype(jnp.float32), (1, 1, 1), "VALID", dimension_numbers=("NCDHW", "OIDHW", "NCDHW"), precision=lax.Precision.HIGHEST)[0, :, 0]
        output = jax.nn.silu(summed + bias_vec[:, None, None]).astype(jnp.bfloat16)
        if head_weight is None:
            return output
        widened = lax.optimization_barrier(output).astype(jnp.float32)
        return jnp.einsum("oc,cxy->oxy", head_weight.astype(jnp.float32), widened, precision=lax.Precision.HIGHEST)

    planes = lax.map(one_plane, jnp.arange(NZ, dtype=jnp.int32))
    return jnp.transpose(planes, (1, 0, 2, 3))


def reference(offsets, particle_mass, velocity, home_cell, home_tile, conv1_weight, conv1_bias, conv2_weight, conv2_bias, head_weight):
    positions = particle_cells(home_cell, home_tile)
    corners = corner_list(positions, offsets)
    values = jnp.concatenate([particle_mass[None], particle_mass[None] * velocity], axis=0)
    mesh_grid = jnp.zeros((PAINTED, NZ * NX * NY), jnp.float32)
    for flat_index, weight in corners:
        mesh_grid = mesh_grid.at[:, flat_index].add(values * weight[None])
    density = mesh_grid.reshape(PAINTED, NZ, NX, NY).astype(jnp.bfloat16)
    hidden = convolve_all(density, conv1_weight, conv1_bias, None)
    force_field = convolve_all(hidden, conv2_weight, conv2_bias, head_weight).reshape(3, NZ * NX * NY)
    forces = jnp.zeros((3, offsets.shape[1]), jnp.float32)
    for flat_index, weight in corners:
        forces = forces + force_field[:, flat_index] * weight[None]
    return forces
```

```python
import functools

import jax
import jax.numpy as jnp
import numpy as np
from jax import lax
from jax.experimental import pallas as pl
from jax.experimental.pallas import tpu as pltpu
from jax.sharding import PartitionSpec as P

TX = 16
TY = 128
TZ = 2
MESH_IDS = pl.DeviceIdType.MESH


def repeat(low, high, body):
    if high - low <= 16:
        for step in range(low, high):
            body(step)
    else:
        lax.fori_loop(low, high, lambda step, carry: (body(step), carry)[1], 0)


def iota(shape, dim):
    return lax.broadcasted_iota(jnp.int32, shape, dim)


class Sizes:
    def __init__(self, mesh_shape, rows):
        self.gx, self.gy, self.gz = (mesh_shape[name] for name in ("gx", "gy", "gz"))
        self.chips = self.gx * self.gy
        self.devices = self.chips * self.gz
        self.nx, self.ny, self.nz = TX * self.gx, TY * self.gy, TZ * self.gz
        self.own = self.nx // self.devices
        self.rows = rows
        self.y_bits = (self.ny - 1).bit_length()
        self.x_bits = (self.nx - 1).bit_length()
        self.flat = -(-self.nz * self.own // 8) * 8
        self.field = -(-3 * self.flat // 16) * 16


def silu(v):
    return v / (1.0 + jnp.exp(-v))


def kernel(
    s,
    off_ref,
    mass_ref,
    vel_ref,
    cell_ref,
    tile_ref,
    w1_ref,
    b1_ref,
    w2_ref,
    b2_ref,
    head_ref,
    out_ref,
    rows_buf,
    field_buf,
    total,
    density,
    hidden,
    features,
    send1,
    recv1,
    relay1,
    send2,
    recv2,
    relay2,
):
    run = lax.axis_index("runs")
    gx = lax.axis_index("gx")
    gy = lax.axis_index("gy")
    gz = lax.axis_index("gz")
    chip = gx * s.gy + gy
    n = s.chips

    def peer(step):
        other = lax.rem(chip + step, n)
        return (run, other // s.gy, lax.rem(other, s.gy), gz)

    sibling = (run, gx, gy, 1 - gz)

    barrier = pltpu.get_barrier_semaphore()

    def greet(step):
        pl.semaphore_signal(barrier, inc=1, device_id=peer(step), device_id_type=MESH_IDS)

    repeat(1, n, greet)
    pl.semaphore_signal(barrier, inc=1, device_id=sibling, device_id_type=MESH_IDS)

    cell = cell_ref[...]
    tile = tile_ref[...]
    negative = jnp.where(off_ref[...] < 0.0, 1, 0).astype(jnp.int32)
    high = jnp.where(off_ref[...] < 0.0, 1.0 + off_ref[...], off_ref[...])
    z_low = gz * TZ + cell // (TX * TY) - negative[0:1]
    x_low = (tile // s.gy) * TX + (cell // TY) % TX - negative[1:2]
    y_low = (tile % s.gy) * TY + cell % TY - negative[2:3]
    x_low = jnp.where(x_low < 0, s.nx - 1, x_low)
    y_low = jnp.where(y_low < 0, s.ny - 1, y_low)
    code = y_low + (x_low << s.y_bits) + ((z_low + 1) << (s.y_bits + s.x_bits))
    mass = mass_ref[...]
    rows_buf[0, 0, 0:1, :] = code.astype(jnp.float32)
    rows_buf[0, 0, 1:4, :] = high
    rows_buf[0, 0, 4:5, :] = mass
    rows_buf[0, 0, 5:8, :] = mass * vel_ref[...]

    pl.semaphore_wait(barrier, n)

    def outgoing(buf, sends, recvs, step):
        return pltpu.make_async_remote_copy(
            src_ref=buf.at[0, 0],
            dst_ref=buf.at[step, 0],
            send_sem=sends.at[step],
            recv_sem=recvs.at[step, 0],
            device_id=peer(step),
            device_id_type=MESH_IDS,
        )

    def passed(buf, relays, recvs, step):
        return pltpu.make_async_remote_copy(
            src_ref=buf.at[step, 0],
            dst_ref=buf.at[step, 1],
            send_sem=relays.at[step],
            recv_sem=recvs.at[step, 1],
            device_id=sibling,
            device_id_type=MESH_IDS,
        )

    def launch(buf, sends, recvs, relays):
        passed(buf, relays, recvs, 0).start()
        repeat(1, n, lambda step: outgoing(buf, sends, recvs, step).start())

    launch(rows_buf, send1, recv1, relay1)

    owner = chip * s.gz + gz
    base = owner * s.own - 2
    base = jnp.where(base < 0, base + s.nx, base)
    width = s.own + 4
    width8 = -(-width // 8) * 8

    def corners(block):
        packed = block[0:1].astype(jnp.int32)
        y = packed & ((1 << s.y_bits) - 1)
        x = (packed >> s.y_bits) & ((1 << s.x_bits) - 1)
        z = (packed >> (s.y_bits + s.x_bits)) - 1
        return z, x, y

    side = 16 * width
    channel = iota((4 * s.nz, s.rows), 0) % 4
    level = iota((4 * s.nz, s.rows), 0) // 4
    x_row = iota((width8, s.rows), 0)
    y_row = iota((s.ny, s.rows), 0)

    def paint(step, core):
        block = rows_buf[step, core]
        z, x, y = corners(block)
        wz, wx, wy = block[1:2], block[2:3], block[3:4]
        value = jnp.where(
            channel == 0,
            block[4:5],
            jnp.where(channel == 1, block[5:6], jnp.where(channel == 2, block[6:7], block[7:8])),
        )
        value = value * jnp.where(level == z, 1.0 - wz, jnp.where(level == z + 1, wz, 0.0))
        low_side = value * (1.0 - wy)
        high_side = value * wy
        x0 = x - base
        x0 = jnp.where(x0 < 0, x0 + s.nx, x0)
        x1 = jnp.where(x0 == s.nx - 1, 0, x0 + 1)
        x_weight = jnp.where(x_row == x0, 1.0 - wx, jnp.where(x_row == x1, wx, 0.0))
        parts = [
            (values * x_weight[j : j + 1]).astype(jnp.bfloat16)
            for values in (low_side, high_side)
            for j in range(width)
        ]
        left = jnp.concatenate(parts, axis=0)
        right = jnp.where(y_row == y, 1.0, 0.0).astype(jnp.bfloat16)
        total[...] += lax.dot_general(
            left, right, (((1,), (1,)), ((), ())), preferred_element_type=jnp.float32
        )

    total[...] = jnp.zeros_like(total)
    paint(0, 0)
    passed(rows_buf, relay1, recv1, 0).wait_recv()
    paint(0, 1)

    def arrive(step):
        outgoing(rows_buf, send1, recv1, step).wait_recv()
        passed(rows_buf, relay1, recv1, step).start()
        paint(step, 0)

    def arrive_relayed(step):
        passed(rows_buf, relay1, recv1, step).wait_recv()
        paint(step, 1)

    repeat(1, n, arrive)
    repeat(1, n, arrive_relayed)

    depth = 4 * s.nz
    half = depth * width
    field = total[0:half, :] + pltpu.roll(total[half : 2 * half, :], 1, 1)
    density[...] = field.astype(jnp.bfloat16)

    wide = 16 * s.nz

    def convolve(weight, source, bias_ref, count):
        products = jnp.dot(weight, source, preferred_element_type=jnp.float32)
        summed = (
            pltpu.roll(products[0:wide], 1, 1)
            + products[wide : 2 * wide]
            + pltpu.roll(products[2 * wide :], s.ny - 1, 1)
        )
        return silu(summed + bias_ref[...]).astype(jnp.bfloat16)

    for j in range(s.own + 2):
        hidden[j * wide : (j + 1) * wide, :] = convolve(
            w1_ref[...], density[j * depth : (j + 3) * depth, :], b1_ref, depth
        )
    for j in range(s.own):
        features[j * wide : (j + 1) * wide, :] = convolve(
            w2_ref[...], hidden[j * wide : (j + 3) * wide, :], b2_ref, wide
        )
    field_buf[0, 0] = jnp.dot(
        head_ref[...], features[...], preferred_element_type=jnp.float32
    ).astype(jnp.bfloat16)

    launch(field_buf, send2, recv2, relay2)

    block = rows_buf[0, 0]
    z, x, y = corners(block)
    wz, wx, wy = block[1:2], block[2:3], block[3:4]
    y_next = jnp.where(y == s.ny - 1, 0, y + 1)
    x_next = jnp.where(x == s.nx - 1, 0, x + 1)
    y_hat = jnp.where(y_row == y, 1.0 - wy, jnp.where(y_row == y_next, wy, 0.0)).astype(
        jnp.bfloat16
    )
    flat_row = iota((s.flat, s.rows), 0)
    flat_z = flat_row // s.own
    flat_x = flat_row % s.own
    z_hat = jnp.where(flat_z == z, 1.0 - wz, jnp.where(flat_z == z + 1, wz, 0.0))

    def gather(step, core):
        source = lax.rem(chip - step + n, n) * s.gz + (gz if core == 0 else 1 - gz)
        shifted = flat_x + source * s.own
        weight = z_hat * jnp.where(
            shifted == x, 1.0 - wx, jnp.where(shifted == x_next, wx, 0.0)
        )
        picked = jnp.dot(field_buf[step, core], y_hat, preferred_element_type=jnp.float32)
        for c in range(3):
            out_ref[c : c + 1, :] += jnp.sum(
                picked[c * s.flat : (c + 1) * s.flat] * weight, axis=0, keepdims=True
            )

    out_ref[...] = jnp.zeros_like(out_ref)
    gather(0, 0)
    passed(field_buf, relay2, recv2, 0).wait_recv()
    gather(0, 1)

    def collect(step):
        outgoing(field_buf, send2, recv2, step).wait_recv()
        passed(field_buf, relay2, recv2, step).start()
        gather(step, 0)

    def collect_relayed(step):
        passed(field_buf, relay2, recv2, step).wait_recv()
        gather(step, 1)

    repeat(1, n, collect)
    repeat(1, n, collect_relayed)

    def finish(step):
        outgoing(rows_buf, send1, recv1, step).wait_send()
        outgoing(field_buf, send2, recv2, step).wait_send()

    def finish_relayed(step):
        passed(rows_buf, relay1, recv1, step).wait_send()
        passed(field_buf, relay2, recv2, step).wait_send()

    repeat(1, n, finish)
    repeat(0, n, finish_relayed)


def banded(weight, nz):
    out_channels, in_channels = weight.shape[:2]
    place = np.zeros((3, nz, nz), np.float32)
    for a in range(3):
        for z in range(nz):
            if 0 <= z + a - 1 < nz:
                place[a, z, z + a - 1] = 1.0
    spread = jnp.einsum("oiabe,azq->ezobqi", weight, jnp.asarray(place, jnp.bfloat16))
    return spread.reshape(3 * nz * out_channels, 3 * nz * in_channels).astype(jnp.bfloat16)


def head_matrix(head_weight, s):
    comps, channels = head_weight.shape
    full = jnp.einsum(
        "co,zw,xv->czxvwo",
        head_weight,
        jnp.eye(s.nz, dtype=jnp.bfloat16),
        jnp.eye(s.own, dtype=jnp.bfloat16),
    ).reshape(comps, s.nz * s.own, s.own * s.nz * channels)
    full = jnp.pad(full, ((0, 0), (0, s.flat - s.nz * s.own), (0, 0)))
    full = full.reshape(comps * s.flat, -1)
    return jnp.pad(full, ((0, s.field - comps * s.flat), (0, 0))).astype(jnp.bfloat16)


def on_device(
    mesh_shape,
    offsets,
    particle_mass,
    velocity,
    home_cell,
    home_tile,
    conv1_weight,
    conv1_bias,
    conv2_weight,
    conv2_bias,
    head_weight,
):
    s = Sizes(mesh_shape, offsets.shape[1])
    w1 = banded(conv1_weight, s.nz)
    w2 = banded(conv2_weight, s.nz)
    b1 = jnp.tile(conv1_bias, s.nz)[:, None]
    b2 = jnp.tile(conv2_bias, s.nz)[:, None]
    head = head_matrix(head_weight, s)
    wide = 16 * s.nz
    depth = 4 * s.nz
    width = s.own + 4
    dma = pltpu.SemaphoreType.DMA
    vmem = pl.BlockSpec(memory_space=pltpu.VMEM)
    return pl.pallas_call(
        functools.partial(kernel, s),
        out_shape=jax.ShapeDtypeStruct((3, s.rows), jnp.float32),
        in_specs=[vmem] * 10,
        out_specs=vmem,
        scratch_shapes=[
            pltpu.VMEM((s.chips, 2, 8, s.rows), jnp.float32),
            pltpu.VMEM((s.chips, 2, s.field, s.ny), jnp.bfloat16),
            pltpu.VMEM((2 * depth * width, s.ny), jnp.float32),
            pltpu.VMEM((depth * width, s.ny), jnp.bfloat16),
            pltpu.VMEM((wide * (s.own + 2), s.ny), jnp.bfloat16),
            pltpu.VMEM((wide * s.own, s.ny), jnp.bfloat16),
            dma((s.chips,)),
            dma((s.chips, 2)),
            dma((s.chips,)),
            dma((s.chips,)),
            dma((s.chips, 2)),
            dma((s.chips,)),
        ],
        compiler_params=pltpu.CompilerParams(
            collective_id=0, has_side_effects=True, vmem_limit_bytes=48 * 1024 * 1024
        ),
    )(
        offsets,
        particle_mass[None],
        velocity,
        home_cell[None],
        home_tile[None],
        w1,
        b1,
        w2,
        b2,
        head,
    )


def solution(mesh):
    rows = P(("runs", "gx", "gy", "gz"))
    columns = P(None, ("runs", "gx", "gy", "gz"))
    in_specs = (columns, rows, columns, rows, rows, P(), P(), P(), P(), P())
    return jax.shard_map(
        functools.partial(on_device, dict(mesh.shape)),
        mesh=mesh,
        in_specs=in_specs,
        out_specs=columns,
        check_vma=False,
    )
```

```python
import functools

import jax
import jax.numpy as jnp
from jax import lax
from jax.experimental import pallas as pl
from jax.experimental.pallas import tpu as pltpu
from jax.sharding import PartitionSpec as P

TX = 16
TY = 128
TZ = 2
MESH_IDS = pl.DeviceIdType.MESH


def repeat(low, high, body):
    if high - low <= 16:
        for step in range(low, high):
            body(step)
    else:
        lax.fori_loop(low, high, lambda step, carry: (body(step), carry)[1], 0)


def iota(shape, dim):
    return lax.broadcasted_iota(jnp.int32, shape, dim)


class Sizes:
    def __init__(self, mesh_shape, rows):
        self.gx, self.gy, self.gz = (mesh_shape[name] for name in ("gx", "gy", "gz"))
        self.chips = self.gx * self.gy
        self.devices = self.chips * self.gz
        self.nx, self.ny, self.nz = TX * self.gx, TY * self.gy, TZ * self.gz
        self.own = self.nx // self.devices
        self.rows = rows
        self.y_bits = (self.ny - 1).bit_length()
        self.x_bits = (self.nx - 1).bit_length()
        self.flat = -(-self.nz * self.own // 8) * 8
        self.field = -(-3 * self.flat // 16) * 16


def silu(v):
    return v / (1.0 + jnp.exp(-v))


def spread_taps(s, taps, in_channels, target):
    columns = 3 * s.nz * in_channels
    group = iota((16, columns), 1) // in_channels
    for e in range(3):
        for z in range(s.nz):
            block = jnp.zeros((16, columns), jnp.float32)
            for a in range(3):
                if 0 <= z + a - 1 < s.nz:
                    for b in range(3):
                        block = jnp.where(
                            group == b * s.nz + z + a - 1, taps((a * 3 + b) * 3 + e), block
                        )
            start = (e * s.nz + z) * 16
            target[start : start + 16, :] = block.astype(jnp.bfloat16)


def copies(rows, columns):
    row = iota((rows, columns), 0)
    return jnp.where(row == iota((rows, columns), 1) % rows, 1.0, 0.0).astype(jnp.bfloat16)


def prepare(s, raw1, bias1, raw2, bias2, head, w1, b1, w2, b2, field_head):
    depth, wide = 4 * s.nz, 16 * s.nz
    four = copies(4, 3 * depth)
    spread_taps(
        s,
        lambda k: lax.dot_general(
            raw1[k], four, (((0,), (0,)), ((), ())), preferred_element_type=jnp.float32
        ),
        4,
        w1,
    )
    taps2 = jnp.dot(raw2[...], copies(16, 3 * wide), preferred_element_type=jnp.float32)
    spread_taps(s, lambda k: taps2[k * 16 : (k + 1) * 16], 16, w2)
    for source, target in ((bias1, b1), (bias2, b2)):
        pick = iota((wide, 16), 0) % 16 == iota((wide, 16), 1)
        target[...] = jnp.sum(jnp.where(pick, source[...], 0.0), axis=1, keepdims=True)
    columns = s.own * wide
    spread = jnp.dot(head[...], copies(16, columns), preferred_element_type=jnp.float32)
    row = iota((s.field, columns), 0)
    lane = iota((s.field, columns), 1)
    component = row // s.flat
    chosen = jnp.where(
        component == 0, spread[0:1], jnp.where(component == 1, spread[1:2], spread[2:3])
    )
    match = (row % s.flat == (lane // 16) % s.nz * s.own + lane // wide) & (component < 3)
    field_head[...] = jnp.where(match, chosen, 0.0).astype(jnp.bfloat16)


def kernel(
    s,
    off_hbm,
    mass_hbm,
    vel_hbm,
    cell_hbm,
    tile_hbm,
    raw1_hbm,
    bias1_hbm,
    raw2_hbm,
    bias2_hbm,
    headw_hbm,
    out_ref,
    off_ref,
    mass_ref,
    vel_ref,
    cell_ref,
    tile_ref,
    raw1_ref,
    bias1_ref,
    raw2_ref,
    bias2_ref,
    headw_ref,
    w1_ref,
    b1_ref,
    w2_ref,
    b2_ref,
    head_ref,
    load_sem,
    rows_buf,
    field_buf,
    total,
    density,
    hidden,
    features,
    send1,
    recv1,
    relay1,
    send2,
    recv2,
    relay2,
):
    run = lax.axis_index("runs")
    gx = lax.axis_index("gx")
    gy = lax.axis_index("gy")
    gz = lax.axis_index("gz")
    chip = gx * s.gy + gy
    n = s.chips

    def peer(step):
        other = lax.rem(chip + step, n)
        return (run, other // s.gy, lax.rem(other, s.gy), gz)

    sibling = (run, gx, gy, 1 - gz)

    barrier = pltpu.get_barrier_semaphore()

    def greet(step):
        pl.semaphore_signal(barrier, inc=1, device_id=peer(step), device_id_type=MESH_IDS)

    repeat(1, n, greet)
    pl.semaphore_signal(barrier, inc=1, device_id=sibling, device_id_type=MESH_IDS)

    loads = [
        pltpu.make_async_copy(source, target, load_sem.at[k])
        for k, (source, target) in enumerate(
            (
                (off_hbm, off_ref),
                (mass_hbm, mass_ref),
                (vel_hbm, vel_ref),
                (cell_hbm, cell_ref),
                (tile_hbm, tile_ref),
                (raw1_hbm, raw1_ref),
                (bias1_hbm, bias1_ref),
                (raw2_hbm, raw2_ref),
                (bias2_hbm, bias2_ref),
                (headw_hbm, headw_ref),
            )
        )
    ]
    for load in loads:
        load.start()
    for load in loads[:5]:
        load.wait()

    cell = cell_ref[...]
    tile = tile_ref[...]
    negative = jnp.where(off_ref[...] < 0.0, 1, 0).astype(jnp.int32)
    high = jnp.where(off_ref[...] < 0.0, 1.0 + off_ref[...], off_ref[...])
    z_low = gz * TZ + cell // (TX * TY) - negative[0:1]
    x_low = (tile // s.gy) * TX + (cell // TY) % TX - negative[1:2]
    y_low = (tile % s.gy) * TY + cell % TY - negative[2:3]
    x_low = jnp.where(x_low < 0, s.nx - 1, x_low)
    y_low = jnp.where(y_low < 0, s.ny - 1, y_low)
    code = y_low + (x_low << s.y_bits) + ((z_low + 1) << (s.y_bits + s.x_bits))
    mass = mass_ref[...]
    rows_buf[0, 0, 0:1, :] = code.astype(jnp.float32)
    rows_buf[0, 0, 1:4, :] = high
    rows_buf[0, 0, 4:5, :] = mass
    rows_buf[0, 0, 5:8, :] = mass * vel_ref[...]

    pl.semaphore_wait(barrier, n)

    def outgoing(buf, sends, recvs, step):
        return pltpu.make_async_remote_copy(
            src_ref=buf.at[0, 0],
            dst_ref=buf.at[step, 0],
            send_sem=sends.at[step],
            recv_sem=recvs.at[step, 0],
            device_id=peer(step),
            device_id_type=MESH_IDS,
        )

    def passed(buf, relays, recvs, step):
        return pltpu.make_async_remote_copy(
            src_ref=buf.at[step, 0],
            dst_ref=buf.at[step, 1],
            send_sem=relays.at[step],
            recv_sem=recvs.at[step, 1],
            device_id=sibling,
            device_id_type=MESH_IDS,
        )

    def launch(buf, sends, recvs, relays):
        passed(buf, relays, recvs, 0).start()
        repeat(1, n, lambda step: outgoing(buf, sends, recvs, step).start())

    launch(rows_buf, send1, recv1, relay1)

    for load in loads[5:]:
        load.wait()
    prepare(s, raw1_ref, bias1_ref, raw2_ref, bias2_ref, headw_ref, w1_ref, b1_ref, w2_ref, b2_ref, head_ref)

    owner = chip * s.gz + gz
    base = owner * s.own - 2
    base = jnp.where(base < 0, base + s.nx, base)
    width = s.own + 4
    width8 = -(-width // 8) * 8

    def corners(block):
        packed = block[0:1].astype(jnp.int32)
        y = packed & ((1 << s.y_bits) - 1)
        x = (packed >> s.y_bits) & ((1 << s.x_bits) - 1)
        z = (packed >> (s.y_bits + s.x_bits)) - 1
        return z, x, y

    side = 16 * width
    channel = iota((4 * s.nz, s.rows), 0) % 4
    level = iota((4 * s.nz, s.rows), 0) // 4
    x_row = iota((width8, s.rows), 0)
    y_row = iota((s.ny, s.rows), 0)

    def paint(step, core):
        block = rows_buf[step, core]
        z, x, y = corners(block)
        wz, wx, wy = block[1:2], block[2:3], block[3:4]
        value = jnp.where(
            channel == 0,
            block[4:5],
            jnp.where(channel == 1, block[5:6], jnp.where(channel == 2, block[6:7], block[7:8])),
        )
        value = value * jnp.where(level == z, 1.0 - wz, jnp.where(level == z + 1, wz, 0.0))
        low_side = value * (1.0 - wy)
        high_side = value * wy
        x0 = x - base
        x0 = jnp.where(x0 < 0, x0 + s.nx, x0)
        x1 = jnp.where(x0 == s.nx - 1, 0, x0 + 1)
        x_weight = jnp.where(x_row == x0, 1.0 - wx, jnp.where(x_row == x1, wx, 0.0))
        parts = [
            (values * x_weight[j : j + 1]).astype(jnp.bfloat16)
            for values in (low_side, high_side)
            for j in range(width)
        ]
        left = jnp.concatenate(parts, axis=0)
        right = jnp.where(y_row == y, 1.0, 0.0).astype(jnp.bfloat16)
        total[...] += lax.dot_general(
            left, right, (((1,), (1,)), ((), ())), preferred_element_type=jnp.float32
        )

    total[...] = jnp.zeros_like(total)
    paint(0, 0)
    passed(rows_buf, relay1, recv1, 0).wait_recv()
    paint(0, 1)

    def arrive(step):
        outgoing(rows_buf, send1, recv1, step).wait_recv()
        passed(rows_buf, relay1, recv1, step).start()
        paint(step, 0)

    def arrive_relayed(step):
        passed(rows_buf, relay1, recv1, step).wait_recv()
        paint(step, 1)

    repeat(1, n, arrive)
    repeat(1, n, arrive_relayed)

    depth = 4 * s.nz
    half = depth * width
    field = total[0:half, :] + pltpu.roll(total[half : 2 * half, :], 1, 1)
    density[...] = field.astype(jnp.bfloat16)

    wide = 16 * s.nz

    def convolve(weight, source, bias_ref, count):
        products = jnp.dot(weight, source, preferred_element_type=jnp.float32)
        summed = (
            pltpu.roll(products[0:wide], 1, 1)
            + products[wide : 2 * wide]
            + pltpu.roll(products[2 * wide :], s.ny - 1, 1)
        )
        return silu(summed + bias_ref[...]).astype(jnp.bfloat16)

    for j in range(s.own + 2):
        hidden[j * wide : (j + 1) * wide, :] = convolve(
            w1_ref[...], density[j * depth : (j + 3) * depth, :], b1_ref, depth
        )
    for j in range(s.own):
        features[j * wide : (j + 1) * wide, :] = convolve(
            w2_ref[...], hidden[j * wide : (j + 3) * wide, :], b2_ref, wide
        )
    field_buf[0, 0] = jnp.dot(
        head_ref[...], features[...], preferred_element_type=jnp.float32
    ).astype(jnp.bfloat16)

    launch(field_buf, send2, recv2, relay2)

    block = rows_buf[0, 0]
    z, x, y = corners(block)
    wz, wx, wy = block[1:2], block[2:3], block[3:4]
    y_next = jnp.where(y == s.ny - 1, 0, y + 1)
    x_next = jnp.where(x == s.nx - 1, 0, x + 1)
    y_hat = jnp.where(y_row == y, 1.0 - wy, jnp.where(y_row == y_next, wy, 0.0)).astype(
        jnp.bfloat16
    )
    flat_row = iota((s.flat, s.rows), 0)
    flat_z = flat_row // s.own
    flat_x = flat_row % s.own
    z_hat = jnp.where(flat_z == z, 1.0 - wz, jnp.where(flat_z == z + 1, wz, 0.0))

    def gather(step, core):
        source = lax.rem(chip - step + n, n) * s.gz + (gz if core == 0 else 1 - gz)
        shifted = flat_x + source * s.own
        weight = z_hat * jnp.where(
            shifted == x, 1.0 - wx, jnp.where(shifted == x_next, wx, 0.0)
        )
        picked = jnp.dot(field_buf[step, core], y_hat, preferred_element_type=jnp.float32)
        for c in range(3):
            out_ref[c : c + 1, :] += jnp.sum(
                picked[c * s.flat : (c + 1) * s.flat] * weight, axis=0, keepdims=True
            )

    out_ref[...] = jnp.zeros_like(out_ref)
    gather(0, 0)
    passed(field_buf, relay2, recv2, 0).wait_recv()
    gather(0, 1)

    def collect(step):
        outgoing(field_buf, send2, recv2, step).wait_recv()
        passed(field_buf, relay2, recv2, step).start()
        gather(step, 0)

    def collect_relayed(step):
        passed(field_buf, relay2, recv2, step).wait_recv()
        gather(step, 1)

    repeat(1, n, collect)
    repeat(1, n, collect_relayed)

    def finish(step):
        outgoing(rows_buf, send1, recv1, step).wait_send()
        outgoing(field_buf, send2, recv2, step).wait_send()

    def finish_relayed(step):
        passed(rows_buf, relay1, recv1, step).wait_send()
        passed(field_buf, relay2, recv2, step).wait_send()

    repeat(1, n, finish)
    repeat(0, n, finish_relayed)


def on_device(
    mesh_shape,
    offsets,
    particle_mass,
    velocity,
    home_cell,
    home_tile,
    conv1_weight,
    conv1_bias,
    conv2_weight,
    conv2_bias,
    head_weight,
):
    s = Sizes(mesh_shape, offsets.shape[1])
    wide = 16 * s.nz
    depth = 4 * s.nz
    width = s.own + 4
    dma = pltpu.SemaphoreType.DMA
    vmem = pl.BlockSpec(memory_space=pltpu.VMEM)
    hbm = pl.BlockSpec(memory_space=pltpu.HBM)
    return pl.pallas_call(
        functools.partial(kernel, s),
        out_shape=jax.ShapeDtypeStruct((3, s.rows), jnp.float32),
        in_specs=[hbm] * 10,
        out_specs=vmem,
        scratch_shapes=[
            pltpu.VMEM((3, s.rows), jnp.float32),
            pltpu.VMEM((1, s.rows), jnp.float32),
            pltpu.VMEM((3, s.rows), jnp.float32),
            pltpu.VMEM((1, s.rows), jnp.int32),
            pltpu.VMEM((1, s.rows), jnp.int32),
            pltpu.VMEM((27, 4, 16), jnp.bfloat16),
            pltpu.VMEM((1, 16), jnp.float32),
            pltpu.VMEM((27 * 16, 16), jnp.bfloat16),
            pltpu.VMEM((1, 16), jnp.float32),
            pltpu.VMEM((3, 16), jnp.bfloat16),
            pltpu.VMEM((3 * wide, 3 * depth), jnp.bfloat16),
            pltpu.VMEM((wide, 1), jnp.float32),
            pltpu.VMEM((3 * wide, 3 * wide), jnp.bfloat16),
            pltpu.VMEM((wide, 1), jnp.float32),
            pltpu.VMEM((s.field, s.own * wide), jnp.bfloat16),
            dma((10,)),
            pltpu.VMEM((s.chips, 2, 8, s.rows), jnp.float32),
            pltpu.VMEM((s.chips, 2, s.field, s.ny), jnp.bfloat16),
            pltpu.VMEM((2 * depth * width, s.ny), jnp.float32),
            pltpu.VMEM((depth * width, s.ny), jnp.bfloat16),
            pltpu.VMEM((wide * (s.own + 2), s.ny), jnp.bfloat16),
            pltpu.VMEM((wide * s.own, s.ny), jnp.bfloat16),
            dma((s.chips,)),
            dma((s.chips, 2)),
            dma((s.chips,)),
            dma((s.chips,)),
            dma((s.chips, 2)),
            dma((s.chips,)),
        ],
        compiler_params=pltpu.CompilerParams(
            collective_id=0, has_side_effects=True, vmem_limit_bytes=62 * 1024 * 1024
        ),
    )(
        offsets,
        particle_mass[None],
        velocity,
        home_cell[None],
        home_tile[None],
        conv1_weight.transpose(2, 3, 4, 1, 0).reshape(27, 4, 16),
        conv1_bias[None],
        conv2_weight.transpose(2, 3, 4, 0, 1).reshape(27 * 16, 16),
        conv2_bias[None],
        head_weight,
    )


def solution(mesh):
    rows = P(("runs", "gx", "gy", "gz"))
    columns = P(None, ("runs", "gx", "gy", "gz"))
    in_specs = (columns, rows, columns, rows, rows, P(), P(), P(), P(), P())
    return jax.shard_map(
        functools.partial(on_device, dict(mesh.shape)),
        mesh=mesh,
        in_specs=in_specs,
        out_specs=columns,
        check_vma=False,
    )
```

```python
import functools

import jax
import jax.numpy as jnp
from jax import lax
from jax.experimental import pallas as pl
from jax.experimental.pallas import tpu as pltpu
from jax.sharding import PartitionSpec as P

TX = 16
TY = 128
TZ = 2
MESH_IDS = pl.DeviceIdType.MESH


def repeat(low, high, body):
    lax.fori_loop(low, high, lambda step, carry: (body(step), carry)[1], 0)


def iota(shape, dim):
    return lax.broadcasted_iota(jnp.int32, shape, dim)


class Sizes:
    def __init__(self, mesh_shape, rows):
        self.gx, self.gy, self.gz = (mesh_shape[name] for name in ("gx", "gy", "gz"))
        self.chips = self.gx * self.gy
        self.devices = self.chips * self.gz
        self.nx, self.ny, self.nz = TX * self.gx, TY * self.gy, TZ * self.gz
        self.own = self.nx // self.devices
        self.rows = rows
        self.y_bits = (self.ny - 1).bit_length()
        self.x_bits = (self.nx - 1).bit_length()
        self.flat = -(-self.nz * self.own // 8) * 8
        self.field = -(-3 * self.flat // 16) * 16


def silu(v):
    return v / (1.0 + jnp.exp(-v))


def spread_taps(s, taps, in_channels, target):
    columns = 3 * s.nz * in_channels
    group = iota((16, columns), 1) // in_channels
    for e in range(3):
        for z in range(s.nz):
            block = jnp.zeros((16, columns), jnp.float32)
            for a in range(3):
                if 0 <= z + a - 1 < s.nz:
                    for b in range(3):
                        block = jnp.where(
                            group == b * s.nz + z + a - 1, taps((a * 3 + b) * 3 + e), block
                        )
            start = (e * s.nz + z) * 16
            target[start : start + 16, :] = block.astype(jnp.bfloat16)


def copies(rows, columns):
    row = iota((rows, columns), 0)
    return jnp.where(row == iota((rows, columns), 1) % rows, 1.0, 0.0).astype(jnp.bfloat16)


def prepare(s, raw1, bias1, raw2, bias2, head, w1, b1, w2, b2, field_head):
    depth, wide = 4 * s.nz, 16 * s.nz
    four = copies(4, 3 * depth)
    spread_taps(
        s,
        lambda k: lax.dot_general(
            raw1[k], four, (((0,), (0,)), ((), ())), preferred_element_type=jnp.float32
        ),
        4,
        w1,
    )
    taps2 = jnp.dot(raw2[...], copies(16, 3 * wide), preferred_element_type=jnp.float32)
    spread_taps(s, lambda k: taps2[k * 16 : (k + 1) * 16], 16, w2)
    for source, target in ((bias1, b1), (bias2, b2)):
        pick = iota((wide, 16), 0) % 16 == iota((wide, 16), 1)
        target[...] = jnp.sum(jnp.where(pick, source[...], 0.0), axis=1, keepdims=True)
    columns = s.own * wide
    spread = jnp.dot(head[...], copies(16, columns), preferred_element_type=jnp.float32)
    row = iota((s.field, columns), 0)
    lane = iota((s.field, columns), 1)
    component = row // s.flat
    chosen = jnp.where(
        component == 0, spread[0:1], jnp.where(component == 1, spread[1:2], spread[2:3])
    )
    match = (row % s.flat == (lane // 16) % s.nz * s.own + lane // wide) & (component < 3)
    field_head[...] = jnp.where(match, chosen, 0.0).astype(jnp.bfloat16)


def kernel(
    s,
    off_hbm,
    mass_hbm,
    vel_hbm,
    cell_hbm,
    tile_hbm,
    raw1_hbm,
    bias1_hbm,
    raw2_hbm,
    bias2_hbm,
    headw_hbm,
    out_ref,
    off_ref,
    mass_ref,
    vel_ref,
    cell_ref,
    tile_ref,
    raw1_ref,
    bias1_ref,
    raw2_ref,
    bias2_ref,
    headw_ref,
    w1_ref,
    b1_ref,
    w2_ref,
    b2_ref,
    head_ref,
    load_sem,
    rows_buf,
    field_buf,
    total,
    density,
    hidden,
    features,
    send1,
    recv1,
    relay1,
    send2,
    recv2,
    relay2,
):
    run = lax.axis_index("runs")
    gx = lax.axis_index("gx")
    gy = lax.axis_index("gy")
    gz = lax.axis_index("gz")
    chip = gx * s.gy + gy
    n = s.chips

    def peer(step):
        other = lax.rem(chip + step, n)
        return (run, other // s.gy, lax.rem(other, s.gy), gz)

    sibling = (run, gx, gy, 1 - gz)

    barrier = pltpu.get_barrier_semaphore()

    def greet(step):
        pl.semaphore_signal(barrier, inc=1, device_id=peer(step), device_id_type=MESH_IDS)

    repeat(1, n, greet)
    pl.semaphore_signal(barrier, inc=1, device_id=sibling, device_id_type=MESH_IDS)

    loads = [
        pltpu.make_async_copy(source, target, load_sem.at[k])
        for k, (source, target) in enumerate(
            (
                (off_hbm, off_ref),
                (mass_hbm, mass_ref),
                (vel_hbm, vel_ref),
                (cell_hbm, cell_ref),
                (tile_hbm, tile_ref),
                (raw1_hbm, raw1_ref),
                (bias1_hbm, bias1_ref),
                (raw2_hbm, raw2_ref),
                (bias2_hbm, bias2_ref),
                (headw_hbm, headw_ref),
            )
        )
    ]
    for load in loads:
        load.start()
    for load in loads[:5]:
        load.wait()

    cell = cell_ref[...]
    tile = tile_ref[...]
    negative = jnp.where(off_ref[...] < 0.0, 1, 0).astype(jnp.int32)
    high = jnp.where(off_ref[...] < 0.0, 1.0 + off_ref[...], off_ref[...])
    z_low = gz * TZ + cell // (TX * TY) - negative[0:1]
    x_low = (tile // s.gy) * TX + (cell // TY) % TX - negative[1:2]
    y_low = (tile % s.gy) * TY + cell % TY - negative[2:3]
    x_low = jnp.where(x_low < 0, s.nx - 1, x_low)
    y_low = jnp.where(y_low < 0, s.ny - 1, y_low)
    code = y_low + (x_low << s.y_bits) + ((z_low + 1) << (s.y_bits + s.x_bits))
    mass = mass_ref[...]
    rows_buf[0, 0, 0:1, :] = code.astype(jnp.float32)
    rows_buf[0, 0, 1:4, :] = high
    rows_buf[0, 0, 4:5, :] = mass
    rows_buf[0, 0, 5:8, :] = mass * vel_ref[...]

    pl.semaphore_wait(barrier, n)

    def outgoing(buf, sends, recvs, step):
        return pltpu.make_async_remote_copy(
            src_ref=buf.at[0, 0],
            dst_ref=buf.at[step, 0],
            send_sem=sends.at[step],
            recv_sem=recvs.at[step, 0],
            device_id=peer(step),
            device_id_type=MESH_IDS,
        )

    def passed(buf, relays, recvs, step):
        return pltpu.make_async_remote_copy(
            src_ref=buf.at[step, 0],
            dst_ref=buf.at[step, 1],
            send_sem=relays.at[step],
            recv_sem=recvs.at[step, 1],
            device_id=sibling,
            device_id_type=MESH_IDS,
        )

    def launch(buf, sends, recvs, relays):
        passed(buf, relays, recvs, 0).start()
        repeat(1, n, lambda step: outgoing(buf, sends, recvs, step).start())

    launch(rows_buf, send1, recv1, relay1)

    for load in loads[5:]:
        load.wait()
    prepare(s, raw1_ref, bias1_ref, raw2_ref, bias2_ref, headw_ref, w1_ref, b1_ref, w2_ref, b2_ref, head_ref)

    owner = chip * s.gz + gz
    base = owner * s.own - 2
    base = jnp.where(base < 0, base + s.nx, base)
    width = s.own + 4
    width8 = -(-width // 8) * 8

    def corners(block):
        packed = block[0:1].astype(jnp.int32)
        y = packed & ((1 << s.y_bits) - 1)
        x = (packed >> s.y_bits) & ((1 << s.x_bits) - 1)
        z = (packed >> (s.y_bits + s.x_bits)) - 1
        return z, x, y

    side = 16 * width
    channel = iota((4 * s.nz, s.rows), 0) % 4
    level = iota((4 * s.nz, s.rows), 0) // 4
    x_row = iota((width8, s.rows), 0)
    y_row = iota((s.ny, s.rows), 0)

    def paint(step, core):
        block = rows_buf[step, core]
        z, x, y = corners(block)
        wz, wx, wy = block[1:2], block[2:3], block[3:4]
        value = jnp.where(
            channel == 0,
            block[4:5],
            jnp.where(channel == 1, block[5:6], jnp.where(channel == 2, block[6:7], block[7:8])),
        )
        value = value * jnp.where(level == z, 1.0 - wz, jnp.where(level == z + 1, wz, 0.0))
        low_side = value * (1.0 - wy)
        high_side = value * wy
        x0 = x - base
        x0 = jnp.where(x0 < 0, x0 + s.nx, x0)
        x1 = jnp.where(x0 == s.nx - 1, 0, x0 + 1)
        x_weight = jnp.where(x_row == x0, 1.0 - wx, jnp.where(x_row == x1, wx, 0.0))
        parts = [
            (values * x_weight[j : j + 1]).astype(jnp.bfloat16)
            for values in (low_side, high_side)
            for j in range(width)
        ]
        left = jnp.concatenate(parts, axis=0)
        right = jnp.where(y_row == y, 1.0, 0.0).astype(jnp.bfloat16)
        total[...] += lax.dot_general(
            left, right, (((1,), (1,)), ((), ())), preferred_element_type=jnp.float32
        )

    total[...] = jnp.zeros_like(total)
    paint(0, 0)
    passed(rows_buf, relay1, recv1, 0).wait_recv()
    paint(0, 1)

    def arrive(step):
        outgoing(rows_buf, send1, recv1, step).wait_recv()
        passed(rows_buf, relay1, recv1, step).start()
        paint(step, 0)

    def arrive_relayed(step):
        passed(rows_buf, relay1, recv1, step).wait_recv()
        paint(step, 1)

    repeat(1, n, arrive)
    repeat(1, n, arrive_relayed)

    depth = 4 * s.nz
    half = depth * width
    field = total[0:half, :] + pltpu.roll(total[half : 2 * half, :], 1, 1)
    density[...] = field.astype(jnp.bfloat16)

    wide = 16 * s.nz

    def convolve(weight, source, bias_ref, count):
        products = jnp.dot(weight, source, preferred_element_type=jnp.float32)
        summed = (
            pltpu.roll(products[0:wide], 1, 1)
            + products[wide : 2 * wide]
            + pltpu.roll(products[2 * wide :], s.ny - 1, 1)
        )
        return silu(summed + bias_ref[...]).astype(jnp.bfloat16)

    for j in range(s.own + 2):
        hidden[j * wide : (j + 1) * wide, :] = convolve(
            w1_ref[...], density[j * depth : (j + 3) * depth, :], b1_ref, depth
        )
    for j in range(s.own):
        features[j * wide : (j + 1) * wide, :] = convolve(
            w2_ref[...], hidden[j * wide : (j + 3) * wide, :], b2_ref, wide
        )
    field_buf[0, 0] = jnp.dot(
        head_ref[...], features[...], preferred_element_type=jnp.float32
    ).astype(jnp.bfloat16)

    launch(field_buf, send2, recv2, relay2)

    block = rows_buf[0, 0]
    z, x, y = corners(block)
    wz, wx, wy = block[1:2], block[2:3], block[3:4]
    y_next = jnp.where(y == s.ny - 1, 0, y + 1)
    x_next = jnp.where(x == s.nx - 1, 0, x + 1)
    y_hat = jnp.where(y_row == y, 1.0 - wy, jnp.where(y_row == y_next, wy, 0.0)).astype(
        jnp.bfloat16
    )
    flat_row = iota((s.flat, s.rows), 0)
    flat_z = flat_row // s.own
    flat_x = flat_row % s.own
    z_hat = jnp.where(flat_z == z, 1.0 - wz, jnp.where(flat_z == z + 1, wz, 0.0))

    def gather(step, core):
        source = lax.rem(chip - step + n, n) * s.gz + (gz if core == 0 else 1 - gz)
        shifted = flat_x + source * s.own
        weight = z_hat * jnp.where(
            shifted == x, 1.0 - wx, jnp.where(shifted == x_next, wx, 0.0)
        )
        picked = jnp.dot(field_buf[step, core], y_hat, preferred_element_type=jnp.float32)
        for c in range(3):
            out_ref[c : c + 1, :] += jnp.sum(
                picked[c * s.flat : (c + 1) * s.flat] * weight, axis=0, keepdims=True
            )

    out_ref[...] = jnp.zeros_like(out_ref)
    gather(0, 0)
    passed(field_buf, relay2, recv2, 0).wait_recv()
    gather(0, 1)

    def collect(step):
        outgoing(field_buf, send2, recv2, step).wait_recv()
        passed(field_buf, relay2, recv2, step).start()
        gather(step, 0)

    def collect_relayed(step):
        passed(field_buf, relay2, recv2, step).wait_recv()
        gather(step, 1)

    repeat(1, n, collect)
    repeat(1, n, collect_relayed)

    def finish(step):
        outgoing(rows_buf, send1, recv1, step).wait_send()
        outgoing(field_buf, send2, recv2, step).wait_send()

    def finish_relayed(step):
        passed(rows_buf, relay1, recv1, step).wait_send()
        passed(field_buf, relay2, recv2, step).wait_send()

    repeat(1, n, finish)
    repeat(0, n, finish_relayed)


def on_device(
    mesh_shape,
    offsets,
    particle_mass,
    velocity,
    home_cell,
    home_tile,
    conv1_weight,
    conv1_bias,
    conv2_weight,
    conv2_bias,
    head_weight,
):
    s = Sizes(mesh_shape, offsets.shape[1])
    wide = 16 * s.nz
    depth = 4 * s.nz
    width = s.own + 4
    dma = pltpu.SemaphoreType.DMA
    vmem = pl.BlockSpec(memory_space=pltpu.VMEM)
    hbm = pl.BlockSpec(memory_space=pltpu.HBM)
    return pl.pallas_call(
        functools.partial(kernel, s),
        out_shape=jax.ShapeDtypeStruct((3, s.rows), jnp.float32),
        in_specs=[hbm] * 10,
        out_specs=vmem,
        scratch_shapes=[
            pltpu.VMEM((3, s.rows), jnp.float32),
            pltpu.VMEM((1, s.rows), jnp.float32),
            pltpu.VMEM((3, s.rows), jnp.float32),
            pltpu.VMEM((1, s.rows), jnp.int32),
            pltpu.VMEM((1, s.rows), jnp.int32),
            pltpu.VMEM((27, 4, 16), jnp.bfloat16),
            pltpu.VMEM((1, 16), jnp.float32),
            pltpu.VMEM((27 * 16, 16), jnp.bfloat16),
            pltpu.VMEM((1, 16), jnp.float32),
            pltpu.VMEM((3, 16), jnp.bfloat16),
            pltpu.VMEM((3 * wide, 3 * depth), jnp.bfloat16),
            pltpu.VMEM((wide, 1), jnp.float32),
            pltpu.VMEM((3 * wide, 3 * wide), jnp.bfloat16),
            pltpu.VMEM((wide, 1), jnp.float32),
            pltpu.VMEM((s.field, s.own * wide), jnp.bfloat16),
            dma((10,)),
            pltpu.VMEM((s.chips, 2, 8, s.rows), jnp.float32),
            pltpu.VMEM((s.chips, 2, s.field, s.ny), jnp.bfloat16),
            pltpu.VMEM((2 * depth * width, s.ny), jnp.float32),
            pltpu.VMEM((depth * width, s.ny), jnp.bfloat16),
            pltpu.VMEM((wide * (s.own + 2), s.ny), jnp.bfloat16),
            pltpu.VMEM((wide * s.own, s.ny), jnp.bfloat16),
            dma((s.chips,)),
            dma((s.chips, 2)),
            dma((s.chips,)),
            dma((s.chips,)),
            dma((s.chips, 2)),
            dma((s.chips,)),
        ],
        compiler_params=pltpu.CompilerParams(
            collective_id=0, has_side_effects=True, vmem_limit_bytes=62 * 1024 * 1024
        ),
    )(
        offsets,
        particle_mass[None],
        velocity,
        home_cell[None],
        home_tile[None],
        conv1_weight.transpose(2, 3, 4, 1, 0).reshape(27, 4, 16),
        conv1_bias[None],
        conv2_weight.transpose(2, 3, 4, 0, 1).reshape(27 * 16, 16),
        conv2_bias[None],
        head_weight,
    )


def solution(mesh):
    rows = P(("runs", "gx", "gy", "gz"))
    columns = P(None, ("runs", "gx", "gy", "gz"))
    in_specs = (columns, rows, columns, rows, rows, P(), P(), P(), P(), P())
    return jax.shard_map(
        functools.partial(on_device, dict(mesh.shape)),
        mesh=mesh,
        in_specs=in_specs,
        out_specs=columns,
        check_vma=False,
    )
```
